32 devices in a mesh: member: 8 (over y, x, core), dp: 4 (over z).
Axes of the slice: x: 2, y: 2, z: 4, core: 2. Of those that a mesh axis runs over, the one named last changes fastest.
Arguments:
- observations: bfloat16 [1024, 1152], P(('member', 'dp')), may hold values from -6 to 6
- rollout: bfloat16 [1024, 384], P(('member', 'dp')), as said below
- done_flags: int32 [1024, 24], P(('member', 'dp')), may hold values 0 or 1
- member_ids: int32 [1024, 1], P(('member', 'dp')), may hold values from 0 to 15; in each aligned block of 32 rows (0 to 31, 32 to 63, ...) at most 6 rows name the same one
- embed_weight: float32 [16, 48, 256], P('member'), may hold values from -0.875 to 0.875
- conv_weight: float32 [16, 3, 2, 256, 256], P('member'), may hold values from -0.25 to 0.25
- trunk_in: float32 [16, 256, 512], P('member'), may hold values from -0.375 to 0.375
- trunk_mid: float32 [16, 512, 512], P('member'), may hold values from -0.25 to 0.25
- head_weight: float32 [16, 512, 13], P('member'), may hold values from -0.15625 to 0.15625
- log_std: float32 [16, 12], P('member'), may hold values from -0.1 to 0.1
Outputs:
- embed_dir: float32 [16, 48, 256], P('member', 'dp')
- conv_dir: float32 [16, 3, 2, 256, 256], P('member', None, None, 'dp')
- in_dir: float32 [16, 256, 512], P('member', 'dp')
- mid_dir: float32 [16, 512, 512], P('member', 'dp')
- head_dir: float32 [16, 512, 13], P('member', 'dp')
- std_dir: float32 [16, 12], P('member')
The draws below stay inside these ranges and needn't reach their ends.
Inputs may be any that keep to these rules, and one draw needn't show every extreme that they name: `member_ids`: in each shard's 32 rows no member is named more than 6 times, a bound that some block reaches. `rollout`: per step: 12 action values, reward, old value, next value, old log-probability.
All inputs are finite; a program needn't handle non-finite values. No bound on the sum of `done_flags` on one device may be relied on, other than what follows from the above.
Results may differ from the reference program's by a relative error of at most 0.023.
Values may be sent and summed in bfloat16 or wider, within the bound.
A program may use at most 128 MiB of HBM per device.

```python
import math
from functools import partial
import jax
import jax.numpy as jnp
import numpy as np
from jax import lax

OBS = 48
STEPS = 24
ACT = 12
CHANNELS = 256
UNITS = 512
LAYERS = 3
CH_DEV = 32
MEMBERS = 16
CAP = 6
ENVS = 1024
PARAMS = 805388
N_MEMBER = 8
N_DP = 4


def draw_rollout(key, part):
    shape = (ENVS, STEPS, ACT + 4)
    base_draw = jax.random.normal(key, shape, jnp.float32)
    actions = base_draw[:, :, :ACT]
    reward = 0.5 * base_draw[:, :, ACT:ACT + 1]
    old_value = base_draw[:, :, ACT + 1:ACT + 2]
    next_value = base_draw[:, :, ACT + 2:ACT + 3]
    old_logp = -0.5 * jnp.sum(actions * actions, axis=2, keepdims=True) - ACT * 0.9189385332046727 + 0.3 * base_draw[:, :, ACT + 3:ACT + 4]
    joined = jnp.concatenate([actions, reward, old_value, next_value, old_logp], axis=2)
    return joined.reshape(ENVS, STEPS * (ACT + 4)).astype(jnp.bfloat16)


def set_ends(array, own_key, least, high):
    index_at = [jax.random.randint(jax.random.fold_in(own_key, axis), (), 0, length) for axis, length in enumerate(array.shape)]
    longest = array.shape.index(max(array.shape))
    next_to = index_at[:longest] + [(index_at[longest] + 1) % array.shape[longest]] + index_at[longest + 1:]
    return array.at[tuple(index_at)].set(least).at[tuple(next_to)].set(high)


def block_scale(stream_key, shape, shards, smallest, largest):
    level, own = 1.0, jax.random.fold_in(stream_key, 6)
    for dim, shards_of in shards:
        steps = jnp.exp(jax.random.uniform(jax.random.fold_in(own, dim), (shards_of,), jnp.float32, smallest / len(shards), largest / len(shards)))
        level = level * jnp.repeat(steps, shape[dim] // shards_of).reshape([-1 if axis == dim else 1 for axis in range(len(shape))])
    return level


def shared_out(key, own, number, rows, count, top, reach, lean):
    ranking = jax.random.permutation(key, count)
    heavy_load, common = load_shares(count, rows * top, reach, lean, True), load_shares(count, rows * top, reach, lean, False)
    places = jnp.arange(count)

    def named(tallies, turn):
        used = int((tallies > 0).sum())
        fixed = max(1, used // 4)
        moved = fixed + (places - fixed + turn * (used - fixed)) % max(1, count - fixed)
        return jnp.zeros((count,), jnp.int32).at[ranking[jnp.where(places < fixed, places, moved)]].set(jnp.asarray(tallies, jnp.int32))

    tallies = jnp.where(number % 4 == 0, named(heavy_load, number // 4), named(common, number - number // 4 - 1))
    mixed = jax.random.permutation(jax.random.fold_in(own, 3), count)
    source_of, receiver = mixed[0:count // 2 * 2:2], mixed[1:count // 2 * 2:2]
    room = jnp.minimum(tallies[source_of] - 1, reach - tallies[receiver]) // 2
    room = jnp.where((source_of == ranking[0]) | (receiver == ranking[0]) | (tallies[receiver] == 0), 0, jnp.maximum(room, 0))
    moved = jax.random.randint(jax.random.fold_in(own, 4), (count // 2,), 0, 1 << 20) % (room + 1)
    tallies = tallies.at[source_of].add(-moved).at[receiver].add(moved)
    members = jnp.searchsorted(jnp.cumsum(tallies), jnp.arange(rows * top), side="right").astype(jnp.int32)
    grid = members.reshape(top, rows).T
    grid = grid[jax.random.permutation(jax.random.fold_in(own, 1), rows)]
    turn = jax.random.randint(jax.random.fold_in(own, 2), (rows, 1), 0, top)
    return jnp.take_along_axis(grid, (jnp.arange(top)[None, :] + turn) % top, axis=1)


def load_shares(count, total, most, slope, full):
    portions = [(1 << 20) // math.isqrt(rank ** slope) + 1 for rank in range(1, count + 1)]
    largest = most if full else min(most, max(-(-total // count), total * portions[0] // sum(portions)))
    least = 1 if total - largest >= count - 1 else 0
    counts, rest = [largest] + [least] * (count - 1), total - largest - least * (count - 1)
    while rest > 0:
        candidates = [i for i in range(1, count) if counts[i] < largest] or [i for i in range(1, count) if counts[i] < most]
        whole, remaining = sum([portions[i] for i in candidates]), rest
        for i in candidates:
            addition = min(most - counts[i], max(1, remaining * portions[i] // whole), rest)
            counts[i] = counts[i] + addition
            rest = rest - addition
    return np.array(counts)


def scatter_about(stream_key, dims, width, most, cuts=(), held_as=jnp.bfloat16):
    values = width * jax.random.normal(stream_key, dims, jnp.float32)
    if cuts:
        values = values * block_scale(stream_key, dims, cuts, -0.22, 0.18)
    return jnp.clip(values, -most, most).astype(held_as)


def setup_inputs(seed: int = 0) -> dict:
    splits = jax.random.split(jax.random.key(seed), 11)
    observations = scatter_about(splits[0], (ENVS, STEPS * OBS), 1.0, 6.0, ((0, 32),))
    rollout = draw_rollout(jax.random.fold_in(splits[10], 71), 0)
    done_flags = set_ends((jax.random.randint(splits[2], (ENVS, STEPS), 0, STEPS) < 1).astype(jnp.int32), jax.random.fold_in(splits[2], 1), 0, 1)
    member_ids_keys = jax.random.split(jax.random.fold_in(splits[3], 1), ENVS // CH_DEV)
    member_ids_turns = jax.random.permutation(jax.random.fold_in(splits[3], 3), ENVS // CH_DEV)
    member_ids = jax.vmap(lambda own, number: shared_out(jax.random.fold_in(splits[3], 2), own, number, CH_DEV, MEMBERS, 1, CAP, 2))(member_ids_keys, member_ids_turns).reshape((ENVS, 1))
    embed_weight = scatter_about(splits[4], (MEMBERS, OBS, CHANNELS), OBS ** -0.5, 0.875, ((0, 8),), jnp.float32)
    conv_weight = scatter_about(splits[5], (MEMBERS, LAYERS, 2, CHANNELS, CHANNELS), (2 * CHANNELS) ** -0.5, 0.25, ((0, 8),), jnp.float32)
    trunk_in = scatter_about(splits[6], (MEMBERS, CHANNELS, UNITS), CHANNELS ** -0.5, 0.375, ((0, 8),), jnp.float32)
    trunk_mid = scatter_about(splits[7], (MEMBERS, UNITS, UNITS), UNITS ** -0.5, 0.25, ((0, 8),), jnp.float32)
    head_weight = scatter_about(splits[8], (MEMBERS, UNITS, ACT + 1), 0.01, 0.15625, ((0, 8),), jnp.float32)
    log_std = jnp.clip(jax.random.uniform(splits[9], (MEMBERS, ACT), jnp.float32, -0.1, 0.1) * block_scale(splits[9], (MEMBERS, ACT), ((0, 8),), -0.4, 0.0), -0.1, 0.1)
    return {"observations": observations, "rollout": rollout, "done_flags": done_flags, "member_ids": member_ids, "embed_weight": embed_weight, "conv_weight": conv_weight, "trunk_in": trunk_in, "trunk_mid": trunk_mid, "head_weight": head_weight, "log_std": log_std}


gamma_rate = 0.99
trace_rate = 0.95
penalty_weight = 0.5
value_weight = 0.5
half_log_tau = 0.9189385332046727

def advantages(reward, old_value, next_value, done_mask):
    alive = 1.0 - done_mask
    td_error = reward + gamma_rate * alive * next_value - old_value
    step_count = td_error.shape[1]
    running = td_error[:, step_count - 1]
    columns = [running]
    for step_index in range(step_count - 2, -1, -1):
        running = td_error[:, step_index] + gamma_rate * trace_rate * alive[:, step_index] * running
        columns.append(running)
    advantage = jnp.stack(columns[::-1], axis=1)
    return (advantage, advantage + old_value)

def policy_loss(weights, observations, rollout, done_mask, live_mask):
    embedding, conv_stack, trunk_first, trunk_second, head_mat, log_scale = weights
    row_count, step_count = done_mask.shape
    channels = embedding.shape[1]
    action_count = log_scale.shape[0]
    features = observations.reshape(row_count * step_count, embedding.shape[0])
    hidden = jnp.dot(features, embedding.astype(jnp.bfloat16), preferred_element_type=jnp.float32)
    for conv_layer in range(conv_stack.shape[0]):
        dilation = 2 ** conv_layer
        current = hidden.astype(jnp.bfloat16)
        shaped = current.reshape(row_count, step_count, channels)
        earlier = jnp.pad(shaped[:, :step_count - dilation], ((0, 0), (dilation, 0), (0, 0)))
        earlier = earlier.reshape(row_count * step_count, channels)
        mixing = jnp.dot(current, conv_stack[conv_layer, 0].astype(jnp.bfloat16), preferred_element_type=jnp.float32)
        mixing = mixing + jnp.dot(earlier, conv_stack[conv_layer, 1].astype(jnp.bfloat16), preferred_element_type=jnp.float32)
        hidden = hidden + jax.nn.elu(mixing)
    trunk_input = hidden.astype(jnp.bfloat16)
    first_units = jax.nn.elu(jnp.dot(trunk_input, trunk_first.astype(jnp.bfloat16), preferred_element_type=jnp.float32)).astype(jnp.bfloat16)
    second = jax.nn.elu(jnp.dot(first_units, trunk_second.astype(jnp.bfloat16), preferred_element_type=jnp.float32)).astype(jnp.bfloat16)
    head_out = jnp.dot(second, head_mat.astype(jnp.bfloat16), preferred_element_type=jnp.float32)
    action_mean = head_out[:, :action_count]
    value_pred = head_out[:, action_count]
    record = rollout.astype(jnp.float32).reshape(row_count, step_count, -1)
    action = record[:, :, :action_count].reshape(row_count * step_count, action_count)
    advantage, target_value = advantages(record[:, :, action_count], record[:, :, action_count + 1], record[:, :, action_count + 2], done_mask)
    old_logp = record[:, :, action_count + 3].reshape(-1)
    scaled = (action - action_mean) * jnp.exp(-log_scale)
    log_prob = lax.optimization_barrier(jnp.sum(-0.5 * scaled * scaled - log_scale, axis=1)) - action_count * half_log_tau
    log_ratio = log_prob - old_logp
    prob_ratio = jnp.exp(log_ratio)
    value_gap = value_pred - target_value.reshape(-1)
    per_step = -prob_ratio * advantage.reshape(-1) + penalty_weight * (prob_ratio - 1.0 - log_ratio) + 0.5 * value_weight * value_gap * value_gap
    weight = (live_mask[:, None] * jnp.ones((1, step_count), jnp.float32)).reshape(-1)
    return jnp.sum(per_step * weight)

def member_grad(weights, observations, rollout, done_mask, live_mask):
    total_loss, pullback = jax.vjp(partial(policy_loss, observations=observations, rollout=rollout, done_mask=done_mask, live_mask=live_mask), weights)
    return pullback(jnp.ones((), jnp.float32))[0]

def reference(observations, rollout, done_flags, member_ids, embed_weight, conv_weight, trunk_in, trunk_mid, head_weight, log_std):
    slot_count = N_MEMBER * CAP
    width_all = N_MEMBER * CH_DEV
    owner_table = member_ids[:, 0].reshape(N_MEMBER, N_DP, CH_DEV).transpose(1, 0, 2).reshape(N_DP, width_all)
    obs_table = observations.reshape(N_MEMBER, N_DP, CH_DEV, -1).transpose(1, 0, 2, 3).reshape(N_DP, width_all, -1)
    record_table = rollout.reshape(N_MEMBER, N_DP, CH_DEV, -1).transpose(1, 0, 2, 3).reshape(N_DP, width_all, -1)
    done_table = done_flags.reshape(N_MEMBER, N_DP, CH_DEV, -1).transpose(1, 0, 2, 3).reshape(N_DP, width_all, -1)
    position = jnp.arange(width_all, dtype=jnp.int32)

    def one_member(member_data):
        member, weights = member_data

        def one_shard(running_sum, shard_data):
            shard_owner, shard_obs, shard_record, shard_done = shard_data
            matches = shard_owner == member
            sort_key = jnp.where(matches, position, position + width_all).astype(jnp.int32)
            ordering = jnp.argsort(sort_key)[:slot_count].astype(jnp.int32)
            live_mask = matches[ordering].astype(jnp.float32)
            grads = member_grad(weights, shard_obs[ordering], shard_record[ordering], shard_done[ordering].astype(jnp.float32), live_mask)
            return (jax.tree.map(lambda running, adding: running + adding, running_sum, grads), None)
        zero_grads = jax.tree.map(jnp.zeros_like, weights)
        summed, unused = lax.scan(one_shard, zero_grads, (owner_table, obs_table, record_table, done_table))
        return summed
    all_weights = (embed_weight, conv_weight, trunk_in, trunk_mid, head_weight, log_std)
    gradients = lax.map(one_member, (jnp.arange(MEMBERS, dtype=jnp.int32), all_weights))
    squares = sum((lax.optimization_barrier(jnp.sum(grad_part * grad_part, axis=tuple(range(1, grad_part.ndim)))) for grad_part in gradients))
    root_mean = jnp.sqrt(squares / PARAMS + 1e-06)
    return tuple((grad_part / root_mean.reshape((-1,) + (1,) * (grad_part.ndim - 1)) for grad_part in gradients))
```

```python
from functools import partial
import math

import jax
import jax.numpy as jnp
from jax import lax
from jax.experimental import pallas as pl
from jax.experimental.pallas import tpu as pltpu
from jax.sharding import PartitionSpec as P

gamma_rate = 0.99
trace_rate = 0.95
half_log_tau = 0.9189385332046727

f32, bf16 = jnp.float32, jnp.bfloat16
LANES = 128
SPANS = 16


def dot(a, b):
    return jnp.dot(a, b, preferred_element_type=f32)


def dot_nt(a, b):
    return lax.dot_general(a, b, (((1,), (1,)), ((), ())), preferred_element_type=f32)


def dot_tn(a, b):
    return lax.dot_general(a, b, (((0,), (0,)), ((), ())), preferred_element_type=f32)


def elu_parts(p):
    slope = jnp.exp(jnp.minimum(p, 0.0))
    return jnp.maximum(p, 0.0) + (slope - 1.0), slope.astype(bf16)


def later(x, rows):
    return jnp.concatenate([jnp.zeros((rows, x.shape[1]), x.dtype), x[: x.shape[0] - rows]], axis=0)


def sooner(x, rows):
    return jnp.concatenate([x[rows:], jnp.zeros((rows, x.shape[1]), x.dtype)], axis=0)


def part_of(index, share):
    if share >= LANES:
        return pl.multiple_of(index * share, LANES), share, 0
    start = index * share
    whole = (start // LANES) * LANES
    return pl.multiple_of(whole, LANES), LANES, pl.multiple_of(start - whole, 8)


def grad_kernel(
    sizes,
    dp_ref,
    slots_ref,
    embed_ref,
    conv_ref,
    first_ref,
    second_ref,
    head_ref,
    std_ref,
    g_embed,
    g_conv,
    g_first,
    g_second,
    g_head,
    g_std,
    g_square,
    packed,
    w_conv,
    w_back,
    w_first,
    w_second,
    saved_hidden,
    saved_first,
    saved_second,
    slopes_conv,
    slopes_first,
    slopes_second,
    a_conv,
    a_first,
    a_second,
    a_head,
    a_embed,
    a_std,
):
    steps, feats, acts, n_dp = sizes
    member = pl.program_id(0)
    index = dp_ref[0]
    slot_count = slots_ref.shape[0]
    step_width = embed_ref.shape[1]
    channels = embed_ref.shape[2]
    units = first_ref.shape[2]
    layers = conv_ref.shape[1]
    room = packed.shape[0]
    tokens = steps * SPANS
    c_start, c_width, c_off = part_of(index, channels // n_dp)
    u_start, u_width, u_off = part_of(index, units // n_dp)

    tail = slots_ref[:, steps * step_width :]
    pick = (lax.broadcasted_iota(jnp.int32, (16, LANES), 1) == steps).astype(bf16)
    owner = dot_nt(pick, tail)
    mine = (owner == (member + 1).astype(f32)).astype(bf16)
    upto = (
        lax.broadcasted_iota(jnp.int32, (slot_count, slot_count), 0)
        <= lax.broadcasted_iota(jnp.int32, (slot_count, slot_count), 1)
    ).astype(bf16)
    place = jnp.where(mine > 0, dot(mine, upto) - 1.0, -1.0)[:1]
    count = jnp.max(place).astype(jnp.int32) + 1
    choose = (
        lax.broadcasted_iota(jnp.int32, (room, slot_count), 0) == place.astype(jnp.int32)
    ).astype(bf16)
    packed[...] = dot(choose, slots_ref[...]).astype(bf16)

    w_embed = embed_ref[0].astype(bf16)
    w_head = head_ref[0].astype(bf16)
    for layer in range(layers):
        w_conv[layer, :channels] = conv_ref[0, layer, 0].astype(bf16)
        w_conv[layer, channels:] = conv_ref[0, layer, 1].astype(bf16)
        w_back[layer, :, :channels] = conv_ref[0, layer, 0].astype(bf16)
        w_back[layer, :, channels:] = conv_ref[0, layer, 1].astype(bf16)
    w_first[...] = first_ref[0].astype(bf16)
    w_second[...] = second_ref[0].astype(bf16)
    for total in (a_conv, a_first, a_second, a_head, a_embed, a_std):
        total[...] = jnp.zeros_like(total)
    scale = std_ref[0]
    inverse = jnp.exp(-scale)

    lane = lax.broadcasted_iota(jnp.int32, (1, step_width), 1)
    is_act = (lane >= feats) & (lane < feats + acts)
    value_lane = feats + acts

    def block(number, unused):
        row = pl.multiple_of(number * SPANS, SPANS)
        spans = packed[pl.ds(row, SPANS), :]
        tok = jnp.concatenate(
            [spans[:, t * step_width : (t + 1) * step_width] for t in range(steps)], axis=0
        )
        hidden = dot(tok, w_embed)
        for layer in range(layers):
            current = hidden.astype(bf16)
            saved_hidden[layer] = current
            both = jnp.concatenate([current, later(current, SPANS * 2**layer)], axis=1)
            grown, slope = elu_parts(dot(both, w_conv[layer]))
            slopes_conv[layer] = slope
            hidden = hidden + grown
        saved_hidden[layers] = hidden.astype(bf16)
        grown, slope = elu_parts(dot(saved_hidden[layers], w_first[...]))
        slopes_first[...] = slope
        saved_first[...] = grown.astype(bf16)
        grown, slope = elu_parts(dot(saved_first[...], w_second[...]))
        slopes_second[...] = slope
        saved_second[...] = grown.astype(bf16)
        out = dot(saved_second[...], w_head)

        record = tok.astype(f32)
        scaled = jnp.where(is_act, (record - out) * inverse, 0.0)
        logp = jnp.sum(-0.5 * scaled * scaled - scale, axis=1, keepdims=True) - acts * half_log_tau
        ratio = jnp.exp(logp - record[:, value_lane + 3 : value_lane + 4])
        old_value = record[:, value_lane + 1 : value_lane + 2]
        done = spans[:, steps * step_width :].astype(f32)
        alive = 1.0 - jnp.concatenate([done[:, t : t + 1] for t in range(steps)], axis=0)
        td_error = (
            record[:, value_lane : value_lane + 1]
            + gamma_rate * alive * record[:, value_lane + 2 : value_lane + 3]
            - old_value
        )
        carry = gamma_rate * trace_rate * alive
        running = td_error[(steps - 1) * SPANS :]
        columns = [running]
        for t in range(steps - 2, -1, -1):
            at = slice(t * SPANS, (t + 1) * SPANS)
            running = td_error[at] + carry[at] * running
            columns.append(running)
        advantage = jnp.concatenate(columns[::-1], axis=0)
        live = (
            lax.rem(lax.broadcasted_iota(jnp.int32, (tokens, 1), 0), SPANS) + number * SPANS < count
        )
        d_logp = jnp.where(live, 0.5 * (ratio - 1.0) - ratio * advantage, 0.0)
        d_value = jnp.where(
            live, 0.5 * (out[:, value_lane : value_lane + 1] - (advantage + old_value)), 0.0
        )
        d_out = jnp.where(
            is_act, d_logp * scaled * inverse, jnp.where(lane == value_lane, d_value, 0.0)
        ).astype(bf16)
        a_std[...] += jnp.sum(
            jnp.where(is_act, d_logp * (scaled * scaled - 1.0), 0.0), axis=0, keepdims=True
        )

        a_head[...] += dot_tn(saved_second[:, pl.ds(u_start, u_width)], d_out)
        d_second = dot_nt(d_out, w_head).astype(bf16) * slopes_second[...]
        a_second[...] += dot_tn(saved_first[:, pl.ds(u_start, u_width)], d_second)
        d_first = dot_nt(d_second, w_second[...]).astype(bf16) * slopes_first[...]
        a_first[...] += dot_tn(saved_hidden[layers, :, pl.ds(c_start, c_width)], d_first)
        d_hidden = dot_nt(d_first, w_first[...])
        for layer in range(layers - 1, -1, -1):
            lag = SPANS * 2**layer
            d_mix = d_hidden.astype(bf16) * slopes_conv[layer]
            d_taps = jnp.concatenate([d_mix, sooner(d_mix, lag)], axis=1)
            a_conv[layer] += dot_tn(saved_hidden[layer, :, pl.ds(c_start, c_width)], d_taps)
            d_hidden = d_hidden + dot_nt(d_taps, w_back[layer])
        a_embed[...] += dot_tn(tok, d_hidden.astype(bf16))
        return unused

    lax.fori_loop(0, (count + SPANS - 1) // SPANS, block, 0)

    c_share, u_share = channels // n_dp, units // n_dp
    squares = jnp.zeros((), f32)

    def keep(ref, at, value):
        ref[at] = value
        return jnp.sum(value * value)

    for layer in range(layers):
        for tap in range(2):
            columns = slice(tap * channels, (tap + 1) * channels)
            part = a_conv[layer, pl.ds(c_off, c_share), columns]
            squares += keep(g_conv, (0, layer, tap), part)
    squares += keep(g_first, 0, a_first[pl.ds(c_off, c_share), :])
    squares += keep(g_second, 0, a_second[pl.ds(u_off, u_share), :])
    squares += keep(g_head, 0, a_head[pl.ds(u_off, u_share), :])
    shared = keep(g_embed, 0, a_embed[:feats, :]) + keep(g_std, 0, a_std[...])
    g_square[...] = jnp.full(g_square.shape, squares + shared / n_dp, f32)


def member_gradients(slots, steps, weights):
    embed_weight, conv_weight, trunk_in, trunk_mid, head_weight, log_std = weights
    n_dp = lax.axis_size("dp")
    index = lax.axis_index("dp").astype(jnp.int32).reshape(1)
    per_group, feats, channels = embed_weight.shape
    layers, units, acts = conv_weight.shape[1], trunk_in.shape[2], log_std.shape[1]
    step_width = (slots.shape[1] - LANES) // steps
    fill = step_width - feats
    embed = jnp.pad(embed_weight, ((0, 0), (0, fill), (0, 0)))
    head = jnp.pad(head_weight, ((0, 0), (0, 0), (feats, fill - acts - 1)))
    scale = jnp.pad(log_std, ((0, 0), (feats, fill - acts)))[:, None, :]
    c_share, u_share = channels // n_dp, units // n_dp
    c_width, u_width = max(c_share, LANES), max(u_share, LANES)
    tokens = steps * SPANS
    room = -(-(slots.shape[0] // per_group) // SPANS) * SPANS

    def per_member(shape):
        zeros = (0,) * (len(shape) - 1)
        return pl.BlockSpec((1,) + tuple(shape[1:]), lambda m: (m,) + zeros)

    out_shapes = [
        (per_group, feats, channels),
        (per_group, layers, 2, c_share, channels),
        (per_group, c_share, units),
        (per_group, u_share, units),
        (per_group, u_share, step_width),
        (per_group, 1, step_width),
        (per_group, 1, LANES),
    ]
    operands = (embed, conv_weight, trunk_in, trunk_mid, head, scale)
    return pl.pallas_call(
        partial(grad_kernel, (steps, feats, acts, n_dp)),
        grid=(per_group,),
        in_specs=[
            pl.BlockSpec(memory_space=pltpu.SMEM),
            pl.BlockSpec(slots.shape, lambda m: (0, 0)),
        ]
        + [per_member(x.shape) for x in operands],
        out_specs=[per_member(s) for s in out_shapes],
        out_shape=[jax.ShapeDtypeStruct(s, f32) for s in out_shapes],
        scratch_shapes=[
            pltpu.VMEM((room, slots.shape[1]), bf16),
            pltpu.VMEM((layers, 2 * channels, channels), bf16),
            pltpu.VMEM((layers, channels, 2 * channels), bf16),
            pltpu.VMEM((channels, units), bf16),
            pltpu.VMEM((units, units), bf16),
            pltpu.VMEM((layers + 1, tokens, channels), bf16),
            pltpu.VMEM((tokens, units), bf16),
            pltpu.VMEM((tokens, units), bf16),
            pltpu.VMEM((layers, tokens, channels), bf16),
            pltpu.VMEM((tokens, units), bf16),
            pltpu.VMEM((tokens, units), bf16),
            pltpu.VMEM((layers, c_width, 2 * channels), f32),
            pltpu.VMEM((c_width, units), f32),
            pltpu.VMEM((u_width, units), f32),
            pltpu.VMEM((u_width, step_width), f32),
            pltpu.VMEM((step_width, channels), f32),
            pltpu.VMEM((1, step_width), f32),
        ],
        compiler_params=pltpu.CompilerParams(vmem_limit_bytes=56 * 2**20),
    )(index, slots, *operands)


def local(
    observations,
    rollout,
    done_flags,
    member_ids,
    embed_weight,
    conv_weight,
    trunk_in,
    trunk_mid,
    head_weight,
    log_std,
):
    groups = lax.axis_size("member")
    per_group = embed_weight.shape[0]
    members = groups * per_group
    local_rows, steps = done_flags.shape
    feats, acts = embed_weight.shape[1], log_std.shape[1]
    capacity = 3 * local_rows // members * per_group
    owner_ids = member_ids[:, 0]
    group_ids = owner_ids // per_group
    same = group_ids[:, None] == group_ids[None, :]
    ahead = jnp.arange(local_rows)[:, None] > jnp.arange(local_rows)[None, :]
    ranking = jnp.sum((same & ahead).astype(jnp.int32), axis=1)
    target = group_ids * capacity + ranking
    dispatch = (jnp.arange(groups * capacity, dtype=jnp.int32)[:, None] == target[None, :]).astype(
        bf16
    )
    rows = jnp.concatenate(
        [
            observations.reshape(local_rows, steps, -1),
            rollout.reshape(local_rows, steps, -1),
        ],
        axis=2,
    ).reshape(local_rows, -1)
    code = (owner_ids % per_group + 1).astype(bf16)[:, None]
    rows = jnp.concatenate(
        [
            rows,
            done_flags.astype(bf16),
            code,
            jnp.zeros((local_rows, LANES - steps - 1), bf16),
        ],
        axis=1,
    )
    sent = dot(dispatch, rows).astype(bf16).reshape(groups, capacity, -1)
    received = lax.all_to_all(sent, "member", split_axis=0, concat_axis=0, tiled=True)
    slots = lax.all_gather(received.reshape(groups * capacity, -1), "dp", axis=0, tiled=True)

    weights = (embed_weight, conv_weight, trunk_in, trunk_mid, head_weight, log_std)
    g_embed, g_conv, g_first, g_second, g_head, g_std, g_square = member_gradients(
        slots, steps, weights
    )
    entries = sum(math.prod(tensor.shape[1:]) for tensor in weights)
    squares = lax.psum(g_square[:, 0, 0], "dp")
    root_mean = jnp.sqrt(squares / entries + 1e-06)
    share = feats // lax.axis_size("dp")
    g_embed = lax.dynamic_slice_in_dim(g_embed, lax.axis_index("dp") * share, share, 1)
    g_head = g_head[:, :, feats : feats + acts + 1]
    g_std = g_std[:, 0, feats : feats + acts]
    return tuple(
        part / root_mean.reshape((-1,) + (1,) * (part.ndim - 1))
        for part in (g_embed, g_conv, g_first, g_second, g_head, g_std)
    )


def solution(mesh):
    placed = (
        P(("member", "dp"), None),
        P(("member", "dp"), None),
        P(("member", "dp"), None),
        P(("member", "dp"), None),
        P("member", None, None),
        P("member", None, None, None, None),
        P("member", None, None),
        P("member", None, None),
        P("member", None, None),
        P("member", None),
    )
    return jax.shard_map(
        local,
        mesh=mesh,
        in_specs=placed,
        out_specs=(
            P("member", "dp", None),
            P("member", None, None, "dp", None),
            P("member", "dp", None),
            P("member", "dp", None),
            P("member", "dp", None),
            P("member", None),
        ),
        check_vma=False,
    )
```

```python
from functools import partial
import math

import jax
import jax.numpy as jnp
from jax import lax
from jax.experimental import pallas as pl
from jax.experimental.pallas import tpu as pltpu
from jax.sharding import PartitionSpec as P

gamma_rate = 0.99
trace_rate = 0.95
half_log_tau = 0.9189385332046727

f32, bf16 = jnp.float32, jnp.bfloat16
LANES = 128
SPANS = 32


def dot(a, b):
    return jnp.dot(a, b, preferred_element_type=f32)


def dot_nt(a, b):
    return lax.dot_general(a, b, (((1,), (1,)), ((), ())), preferred_element_type=f32)


def dot_tn(a, b):
    return lax.dot_general(a, b, (((0,), (0,)), ((), ())), preferred_element_type=f32)


def elu_parts(p):
    slope = jnp.exp(jnp.minimum(p, 0.0))
    return jnp.maximum(p, 0.0) + (slope - 1.0), slope.astype(bf16)


def later(x, rows):
    return jnp.concatenate([jnp.zeros((rows, x.shape[1]), x.dtype), x[: x.shape[0] - rows]], axis=0)


def sooner(x, rows):
    return jnp.concatenate([x[rows:], jnp.zeros((rows, x.shape[1]), x.dtype)], axis=0)


def part_of(index, share):
    if share >= LANES:
        return pl.multiple_of(index * share, LANES), share, 0
    start = index * share
    whole = (start // LANES) * LANES
    return pl.multiple_of(whole, LANES), LANES, pl.multiple_of(start - whole, 8)


def grad_kernel(
    sizes,
    dp_ref,
    slots_ref,
    embed_ref,
    conv_ref,
    first_ref,
    second_ref,
    head_ref,
    std_ref,
    g_embed,
    g_conv,
    g_first,
    g_second,
    g_head,
    g_std,
    g_square,
    packed,
    w_conv,
    w_back,
    w_first,
    w_second,
    saved_hidden,
    saved_first,
    saved_second,
    slopes_conv,
    slopes_first,
    slopes_second,
    a_conv,
    a_first,
    a_second,
    a_head,
    a_embed,
    a_std,
):
    steps, feats, acts, n_dp = sizes
    member = pl.program_id(0)
    index = dp_ref[0]
    slot_count = slots_ref.shape[0]
    step_width = embed_ref.shape[1]
    channels = embed_ref.shape[2]
    units = first_ref.shape[2]
    layers = conv_ref.shape[1]
    room = packed.shape[0]
    tokens = steps * SPANS
    c_start, c_width, c_off = part_of(index, channels // n_dp)
    u_start, u_width, u_off = part_of(index, units // n_dp)

    tail = slots_ref[:, steps * step_width :]
    pick = (lax.broadcasted_iota(jnp.int32, (16, LANES), 1) == steps).astype(bf16)
    owner = dot_nt(pick, tail)
    mine = (owner == (member + 1).astype(f32)).astype(bf16)
    upto = (
        lax.broadcasted_iota(jnp.int32, (slot_count, slot_count), 0)
        <= lax.broadcasted_iota(jnp.int32, (slot_count, slot_count), 1)
    ).astype(bf16)
    place = jnp.where(mine > 0, dot(mine, upto) - 1.0, -1.0)[:1]
    count = jnp.max(place).astype(jnp.int32) + 1
    choose = (
        lax.broadcasted_iota(jnp.int32, (room, slot_count), 0) == place.astype(jnp.int32)
    ).astype(bf16)
    packed[...] = dot(choose, slots_ref[...]).astype(bf16)

    w_embed = embed_ref[0].astype(bf16)
    w_head = head_ref[0].astype(bf16)
    for layer in range(layers):
        w_conv[layer, :channels] = conv_ref[0, layer, 0].astype(bf16)
        w_conv[layer, channels:] = conv_ref[0, layer, 1].astype(bf16)
        w_back[layer, :, :channels] = conv_ref[0, layer, 0].astype(bf16)
        w_back[layer, :, channels:] = conv_ref[0, layer, 1].astype(bf16)
    w_first[...] = first_ref[0].astype(bf16)
    w_second[...] = second_ref[0].astype(bf16)
    for total in (a_conv, a_first, a_second, a_head, a_embed, a_std):
        total[...] = jnp.zeros_like(total)
    scale = std_ref[0]
    inverse = jnp.exp(-scale)

    lane = lax.broadcasted_iota(jnp.int32, (1, step_width), 1)
    is_act = (lane >= feats) & (lane < feats + acts)
    value_lane = feats + acts

    def block(number, unused):
        row = pl.multiple_of(number * SPANS, SPANS)
        spans = packed[pl.ds(row, SPANS), :]
        tok = jnp.concatenate(
            [spans[:, t * step_width : (t + 1) * step_width] for t in range(steps)], axis=0
        )
        hidden = dot(tok, w_embed)
        for layer in range(layers):
            current = hidden.astype(bf16)
            saved_hidden[layer] = current
            both = jnp.concatenate([current, later(current, SPANS * 2**layer)], axis=1)
            grown, slope = elu_parts(dot(both, w_conv[layer]))
            slopes_conv[layer] = slope
            hidden = hidden + grown
        saved_hidden[layers] = hidden.astype(bf16)
        grown, slope = elu_parts(dot(saved_hidden[layers], w_first[...]))
        slopes_first[...] = slope
        saved_first[...] = grown.astype(bf16)
        grown, slope = elu_parts(dot(saved_first[...], w_second[...]))
        slopes_second[...] = slope
        saved_second[...] = grown.astype(bf16)
        out = dot(saved_second[...], w_head)

        record = tok.astype(f32)
        scaled = jnp.where(is_act, (record - out) * inverse, 0.0)
        logp = jnp.sum(-0.5 * scaled * scaled - scale, axis=1, keepdims=True) - acts * half_log_tau
        ratio = jnp.exp(logp - record[:, value_lane + 3 : value_lane + 4])
        old_value = record[:, value_lane + 1 : value_lane + 2]
        done = spans[:, steps * step_width :].astype(f32)
        alive = 1.0 - jnp.concatenate([done[:, t : t + 1] for t in range(steps)], axis=0)
        td_error = (
            record[:, value_lane : value_lane + 1]
            + gamma_rate * alive * record[:, value_lane + 2 : value_lane + 3]
            - old_value
        )
        carry = gamma_rate * trace_rate * alive
        running = td_error[(steps - 1) * SPANS :]
        columns = [running]
        for t in range(steps - 2, -1, -1):
            at = slice(t * SPANS, (t + 1) * SPANS)
            running = td_error[at] + carry[at] * running
            columns.append(running)
        advantage = jnp.concatenate(columns[::-1], axis=0)
        live = (
            lax.rem(lax.broadcasted_iota(jnp.int32, (tokens, 1), 0), SPANS) + number * SPANS < count
        )
        d_logp = jnp.where(live, 0.5 * (ratio - 1.0) - ratio * advantage, 0.0)
        d_value = jnp.where(
            live, 0.5 * (out[:, value_lane : value_lane + 1] - (advantage + old_value)), 0.0
        )
        d_out = jnp.where(
            is_act, d_logp * scaled * inverse, jnp.where(lane == value_lane, d_value, 0.0)
        ).astype(bf16)
        a_std[...] += jnp.sum(
            jnp.where(is_act, d_logp * (scaled * scaled - 1.0), 0.0), axis=0, keepdims=True
        )

        a_head[...] += dot_tn(saved_second[:, pl.ds(u_start, u_width)], d_out)
        d_second = dot_nt(d_out, w_head).astype(bf16) * slopes_second[...]
        a_second[...] += dot_tn(saved_first[:, pl.ds(u_start, u_width)], d_second)
        d_first = dot_nt(d_second, w_second[...]).astype(bf16) * slopes_first[...]
        a_first[...] += dot_tn(saved_hidden[layers, :, pl.ds(c_start, c_width)], d_first)
        d_hidden = dot_nt(d_first, w_first[...])
        for layer in range(layers - 1, -1, -1):
            lag = SPANS * 2**layer
            d_mix = d_hidden.astype(bf16) * slopes_conv[layer]
            d_taps = jnp.concatenate([d_mix, sooner(d_mix, lag)], axis=1)
            a_conv[layer] += dot_tn(saved_hidden[layer, :, pl.ds(c_start, c_width)], d_taps)
            d_hidden = d_hidden + dot_nt(d_taps, w_back[layer])
        a_embed[...] += dot_tn(tok, d_hidden.astype(bf16))
        return unused

    lax.fori_loop(0, (count + SPANS - 1) // SPANS, block, 0)

    c_share, u_share = channels // n_dp, units // n_dp
    squares = jnp.zeros((), f32)

    def keep(ref, at, value):
        ref[at] = value
        return jnp.sum(value * value)

    for layer in range(layers):
        for tap in range(2):
            columns = slice(tap * channels, (tap + 1) * channels)
            part = a_conv[layer, pl.ds(c_off, c_share), columns]
            squares += keep(g_conv, (0, layer, tap), part)
    squares += keep(g_first, 0, a_first[pl.ds(c_off, c_share), :])
    squares += keep(g_second, 0, a_second[pl.ds(u_off, u_share), :])
    squares += keep(g_head, 0, a_head[pl.ds(u_off, u_share), :])
    shared = keep(g_embed, 0, a_embed[:feats, :]) + keep(g_std, 0, a_std[...])
    g_square[...] = jnp.full(g_square.shape, squares + shared / n_dp, f32)


def member_gradients(slots, steps, weights):
    embed_weight, conv_weight, trunk_in, trunk_mid, head_weight, log_std = weights
    n_dp = lax.axis_size("dp")
    index = lax.axis_index("dp").astype(jnp.int32).reshape(1)
    per_group, feats, channels = embed_weight.shape
    layers, units, acts = conv_weight.shape[1], trunk_in.shape[2], log_std.shape[1]
    step_width = (slots.shape[1] - LANES) // steps
    fill = step_width - feats
    embed = jnp.pad(embed_weight, ((0, 0), (0, fill), (0, 0)))
    head = jnp.pad(head_weight, ((0, 0), (0, 0), (feats, fill - acts - 1)))
    scale = jnp.pad(log_std, ((0, 0), (feats, fill - acts)))[:, None, :]
    c_share, u_share = channels // n_dp, units // n_dp
    c_width, u_width = max(c_share, LANES), max(u_share, LANES)
    tokens = steps * SPANS
    room = -(-(slots.shape[0] // per_group) // SPANS) * SPANS

    def per_member(shape):
        zeros = (0,) * (len(shape) - 1)
        return pl.BlockSpec((1,) + tuple(shape[1:]), lambda m: (m,) + zeros)

    out_shapes = [
        (per_group, feats, channels),
        (per_group, layers, 2, c_share, channels),
        (per_group, c_share, units),
        (per_group, u_share, units),
        (per_group, u_share, step_width),
        (per_group, 1, step_width),
        (per_group, 1, LANES),
    ]
    operands = (embed, conv_weight, trunk_in, trunk_mid, head, scale)
    return pl.pallas_call(
        partial(grad_kernel, (steps, feats, acts, n_dp)),
        grid=(per_group,),
        in_specs=[
            pl.BlockSpec(memory_space=pltpu.SMEM),
            pl.BlockSpec(slots.shape, lambda m: (0, 0)),
        ]
        + [per_member(x.shape) for x in operands],
        out_specs=[per_member(s) for s in out_shapes],
        out_shape=[jax.ShapeDtypeStruct(s, f32) for s in out_shapes],
        scratch_shapes=[
            pltpu.VMEM((room, slots.shape[1]), bf16),
            pltpu.VMEM((layers, 2 * channels, channels), bf16),
            pltpu.VMEM((layers, channels, 2 * channels), bf16),
            pltpu.VMEM((channels, units), bf16),
            pltpu.VMEM((units, units), bf16),
            pltpu.VMEM((layers + 1, tokens, channels), bf16),
            pltpu.VMEM((tokens, units), bf16),
            pltpu.VMEM((tokens, units), bf16),
            pltpu.VMEM((layers, tokens, channels), bf16),
            pltpu.VMEM((tokens, units), bf16),
            pltpu.VMEM((tokens, units), bf16),
            pltpu.VMEM((layers, c_width, 2 * channels), f32),
            pltpu.VMEM((c_width, units), f32),
            pltpu.VMEM((u_width, units), f32),
            pltpu.VMEM((u_width, step_width), f32),
            pltpu.VMEM((step_width, channels), f32),
            pltpu.VMEM((1, step_width), f32),
        ],
        compiler_params=pltpu.CompilerParams(vmem_limit_bytes=56 * 2**20),
    )(index, slots, *operands)


def local(
    observations,
    rollout,
    done_flags,
    member_ids,
    embed_weight,
    conv_weight,
    trunk_in,
    trunk_mid,
    head_weight,
    log_std,
):
    groups = lax.axis_size("member")
    per_group = embed_weight.shape[0]
    members = groups * per_group
    local_rows, steps = done_flags.shape
    feats, acts = embed_weight.shape[1], log_std.shape[1]
    capacity = 3 * local_rows // members * per_group
    owner_ids = member_ids[:, 0]
    group_ids = owner_ids // per_group
    same = group_ids[:, None] == group_ids[None, :]
    ahead = jnp.arange(local_rows)[:, None] > jnp.arange(local_rows)[None, :]
    ranking = jnp.sum((same & ahead).astype(jnp.int32), axis=1)
    target = group_ids * capacity + ranking
    dispatch = (jnp.arange(groups * capacity, dtype=jnp.int32)[:, None] == target[None, :]).astype(
        bf16
    )
    rows = jnp.concatenate(
        [
            observations.reshape(local_rows, steps, -1),
            rollout.reshape(local_rows, steps, -1),
        ],
        axis=2,
    ).reshape(local_rows, -1)
    code = (owner_ids % per_group + 1).astype(bf16)[:, None]
    rows = jnp.concatenate(
        [
            rows,
            done_flags.astype(bf16),
            code,
            jnp.zeros((local_rows, LANES - steps - 1), bf16),
        ],
        axis=1,
    )
    sent = dot(dispatch, rows).astype(bf16).reshape(groups, capacity, -1)
    received = lax.all_to_all(sent, "member", split_axis=0, concat_axis=0, tiled=True)
    slots = lax.all_gather(received.reshape(groups * capacity, -1), "dp", axis=0, tiled=True)

    weights = (embed_weight, conv_weight, trunk_in, trunk_mid, head_weight, log_std)
    g_embed, g_conv, g_first, g_second, g_head, g_std, g_square = member_gradients(
        slots, steps, weights
    )
    entries = sum(math.prod(tensor.shape[1:]) for tensor in weights)
    squares = lax.psum(g_square[:, 0, 0], "dp")
    root_mean = jnp.sqrt(squares / entries + 1e-06)
    share = feats // lax.axis_size("dp")
    g_embed = lax.dynamic_slice_in_dim(g_embed, lax.axis_index("dp") * share, share, 1)
    g_head = g_head[:, :, feats : feats + acts + 1]
    g_std = g_std[:, 0, feats : feats + acts]
    return tuple(
        part / root_mean.reshape((-1,) + (1,) * (part.ndim - 1))
        for part in (g_embed, g_conv, g_first, g_second, g_head, g_std)
    )


def solution(mesh):
    placed = (
        P(("member", "dp"), None),
        P(("member", "dp"), None),
        P(("member", "dp"), None),
        P(("member", "dp"), None),
        P("member", None, None),
        P("member", None, None, None, None),
        P("member", None, None),
        P("member", None, None),
        P("member", None, None),
        P("member", None),
    )
    return jax.shard_map(
        local,
        mesh=mesh,
        in_specs=placed,
        out_specs=(
            P("member", "dp", None),
            P("member", None, None, "dp", None),
            P("member", "dp", None),
            P("member", "dp", None),
            P("member", "dp", None),
            P("member", None),
        ),
        check_vma=False,
    )
```

```python
from functools import partial
import math

import jax
import jax.numpy as jnp
from jax import lax
from jax.experimental import pallas as pl
from jax.experimental.pallas import tpu as pltpu
from jax.sharding import PartitionSpec as P

gamma_rate = 0.99
trace_rate = 0.95
half_log_tau = 0.9189385332046727

f32, bf16 = jnp.float32, jnp.bfloat16
LANES = 128
SPANS = 32


def dot(a, b):
    return jnp.dot(a, b, preferred_element_type=f32)


def dot_nt(a, b):
    return lax.dot_general(a, b, (((1,), (1,)), ((), ())), preferred_element_type=f32)


def dot_tn(a, b):
    return lax.dot_general(a, b, (((0,), (0,)), ((), ())), preferred_element_type=f32)


def elu_parts(p):
    slope = jnp.exp(jnp.minimum(p, 0.0))
    return jnp.maximum(p, 0.0) + (slope - 1.0), slope.astype(bf16)


def later(x, rows):
    return jnp.concatenate([jnp.zeros((rows, x.shape[1]), x.dtype), x[: x.shape[0] - rows]], axis=0)


def sooner(x, rows):
    return jnp.concatenate([x[rows:], jnp.zeros((rows, x.shape[1]), x.dtype)], axis=0)


def part_of(index, share):
    if share >= LANES:
        return pl.multiple_of(index * share, LANES), share, 0
    start = index * share
    whole = (start // LANES) * LANES
    return pl.multiple_of(whole, LANES), LANES, pl.multiple_of(start - whole, 8)


def grad_kernel(
    sizes,
    dp_ref,
    slots_ref,
    embed_ref,
    conv_ref,
    first_ref,
    second_ref,
    head_ref,
    std_ref,
    g_embed,
    g_conv,
    g_first,
    g_second,
    g_head,
    g_std,
    g_square,
    packed,
    w_conv,
    w_back,
    w_first,
    w_second,
    saved_hidden,
    saved_first,
    saved_second,
    slopes_conv,
    slopes_first,
    slopes_second,
    a_conv,
    a_first,
    a_second,
    a_head,
    a_embed,
    a_std,
):
    steps, feats, acts, n_dp = sizes
    member = pl.program_id(0)
    index = dp_ref[0]
    slot_count = slots_ref.shape[0]
    step_width = embed_ref.shape[1]
    channels = embed_ref.shape[2]
    units = first_ref.shape[2]
    layers = conv_ref.shape[1]
    room = packed.shape[0]
    tokens = steps * SPANS
    c_start, c_width, c_off = part_of(index, channels // n_dp)
    u_start, u_width, u_off = part_of(index, units // n_dp)

    tail = slots_ref[:, steps * step_width :]
    lanes = lax.broadcasted_iota(jnp.int32, (16, LANES), 1)
    owner = dot_nt((lanes == steps).astype(bf16), tail)
    used = dot_nt((lanes == steps + 1).astype(bf16), tail)
    wanted = (dp_ref[1] + member).astype(f32)
    mine = jnp.where((owner == wanted) & (used > 0.5), 1.0, 0.0).astype(bf16)
    upto = (
        lax.broadcasted_iota(jnp.int32, (slot_count, slot_count), 0)
        <= lax.broadcasted_iota(jnp.int32, (slot_count, slot_count), 1)
    ).astype(bf16)
    place = jnp.where(mine > 0, dot(mine, upto) - 1.0, -1.0)[:1]
    count = jnp.max(place).astype(jnp.int32) + 1
    choose = (
        lax.broadcasted_iota(jnp.int32, (room, slot_count), 0) == place.astype(jnp.int32)
    ).astype(bf16)
    packed[...] = dot(choose, slots_ref[...]).astype(bf16)

    w_embed = embed_ref[0].astype(bf16)
    w_head = head_ref[0].astype(bf16)
    for layer in range(layers):
        w_conv[layer, :channels] = conv_ref[0, layer, 0].astype(bf16)
        w_conv[layer, channels:] = conv_ref[0, layer, 1].astype(bf16)
        w_back[layer, :, :channels] = conv_ref[0, layer, 0].astype(bf16)
        w_back[layer, :, channels:] = conv_ref[0, layer, 1].astype(bf16)
    w_first[...] = first_ref[0].astype(bf16)
    w_second[...] = second_ref[0].astype(bf16)
    for total in (a_conv, a_first, a_second, a_head, a_embed, a_std):
        total[...] = jnp.zeros_like(total)
    scale = std_ref[0]
    inverse = jnp.exp(-scale)

    lane = lax.broadcasted_iota(jnp.int32, (1, step_width), 1)
    is_act = (lane >= feats) & (lane < feats + acts)
    value_lane = feats + acts

    def block(number, unused):
        row = pl.multiple_of(number * SPANS, SPANS)
        spans = packed[pl.ds(row, SPANS), :]
        tok = jnp.concatenate(
            [spans[:, t * step_width : (t + 1) * step_width] for t in range(steps)], axis=0
        )
        hidden = dot(tok, w_embed)
        for layer in range(layers):
            current = hidden.astype(bf16)
            saved_hidden[layer] = current
            both = jnp.concatenate([current, later(current, SPANS * 2**layer)], axis=1)
            grown, slope = elu_parts(dot(both, w_conv[layer]))
            slopes_conv[layer] = slope
            hidden = hidden + grown
        saved_hidden[layers] = hidden.astype(bf16)
        grown, slope = elu_parts(dot(saved_hidden[layers], w_first[...]))
        slopes_first[...] = slope
        saved_first[...] = grown.astype(bf16)
        grown, slope = elu_parts(dot(saved_first[...], w_second[...]))
        slopes_second[...] = slope
        saved_second[...] = grown.astype(bf16)
        out = dot(saved_second[...], w_head)

        record = tok.astype(f32)
        scaled = jnp.where(is_act, (record - out) * inverse, 0.0)
        logp = jnp.sum(-0.5 * scaled * scaled - scale, axis=1, keepdims=True) - acts * half_log_tau
        ratio = jnp.exp(logp - record[:, value_lane + 3 : value_lane + 4])
        old_value = record[:, value_lane + 1 : value_lane + 2]
        done = spans[:, steps * step_width :].astype(f32)
        alive = 1.0 - jnp.concatenate([done[:, t : t + 1] for t in range(steps)], axis=0)
        td_error = (
            record[:, value_lane : value_lane + 1]
            + gamma_rate * alive * record[:, value_lane + 2 : value_lane + 3]
            - old_value
        )
        carry = gamma_rate * trace_rate * alive
        running = td_error[(steps - 1) * SPANS :]
        columns = [running]
        for t in range(steps - 2, -1, -1):
            at = slice(t * SPANS, (t + 1) * SPANS)
            running = td_error[at] + carry[at] * running
            columns.append(running)
        advantage = jnp.concatenate(columns[::-1], axis=0)
        live = (
            lax.rem(lax.broadcasted_iota(jnp.int32, (tokens, 1), 0), SPANS) + number * SPANS < count
        )
        d_logp = jnp.where(live, 0.5 * (ratio - 1.0) - ratio * advantage, 0.0)
        d_value = jnp.where(
            live, 0.5 * (out[:, value_lane : value_lane + 1] - (advantage + old_value)), 0.0
        )
        d_out = jnp.where(
            is_act, d_logp * scaled * inverse, jnp.where(lane == value_lane, d_value, 0.0)
        ).astype(bf16)
        a_std[...] += jnp.sum(
            jnp.where(is_act, d_logp * (scaled * scaled - 1.0), 0.0), axis=0, keepdims=True
        )

        a_head[...] += dot_tn(saved_second[:, pl.ds(u_start, u_width)], d_out)
        d_second = dot_nt(d_out, w_head).astype(bf16) * slopes_second[...]
        a_second[...] += dot_tn(saved_first[:, pl.ds(u_start, u_width)], d_second)
        d_first = dot_nt(d_second, w_second[...]).astype(bf16) * slopes_first[...]
        a_first[...] += dot_tn(saved_hidden[layers, :, pl.ds(c_start, c_width)], d_first)
        d_hidden = dot_nt(d_first, w_first[...])
        for layer in range(layers - 1, -1, -1):
            lag = SPANS * 2**layer
            d_mix = d_hidden.astype(bf16) * slopes_conv[layer]
            d_taps = jnp.concatenate([d_mix, sooner(d_mix, lag)], axis=1)
            a_conv[layer] += dot_tn(saved_hidden[layer, :, pl.ds(c_start, c_width)], d_taps)
            d_hidden = d_hidden + dot_nt(d_taps, w_back[layer])
        a_embed[...] += dot_tn(tok, d_hidden.astype(bf16))
        return unused

    lax.fori_loop(0, (count + SPANS - 1) // SPANS, block, 0)

    c_share, u_share = channels // n_dp, units // n_dp
    squares = jnp.zeros((), f32)

    def keep(ref, at, value):
        ref[at] = value
        return jnp.sum(value * value)

    for layer in range(layers):
        for tap in range(2):
            columns = slice(tap * channels, (tap + 1) * channels)
            part = a_conv[layer, pl.ds(c_off, c_share), columns]
            squares += keep(g_conv, (0, layer, tap), part)
    squares += keep(g_first, 0, a_first[pl.ds(c_off, c_share), :])
    squares += keep(g_second, 0, a_second[pl.ds(u_off, u_share), :])
    squares += keep(g_head, 0, a_head[pl.ds(u_off, u_share), :])
    shared = keep(g_embed, 0, a_embed[:feats, :]) + keep(g_std, 0, a_std[...])
    g_square[...] = jnp.full(g_square.shape, squares + shared / n_dp, f32)


def member_gradients(slots, steps, weights):
    embed_weight, conv_weight, trunk_in, trunk_mid, head_weight, log_std = weights
    n_dp = lax.axis_size("dp")
    per_group, feats, channels = embed_weight.shape
    index = jnp.stack([lax.axis_index("dp"), lax.axis_index("member") * per_group]).astype(jnp.int32)
    layers, units, acts = conv_weight.shape[1], trunk_in.shape[2], log_std.shape[1]
    step_width = (slots.shape[1] - LANES) // steps
    fill = step_width - feats
    embed = jnp.pad(embed_weight, ((0, 0), (0, fill), (0, 0)))
    head = jnp.pad(head_weight, ((0, 0), (0, 0), (feats, fill - acts - 1)))
    scale = jnp.pad(log_std, ((0, 0), (feats, fill - acts)))[:, None, :]
    c_share, u_share = channels // n_dp, units // n_dp
    c_width, u_width = max(c_share, LANES), max(u_share, LANES)
    tokens = steps * SPANS
    room = -(-(slots.shape[0] // per_group) // SPANS) * SPANS

    def per_member(shape):
        zeros = (0,) * (len(shape) - 1)
        return pl.BlockSpec((1,) + tuple(shape[1:]), lambda m: (m,) + zeros)

    out_shapes = [
        (per_group, feats, channels),
        (per_group, layers, 2, c_share, channels),
        (per_group, c_share, units),
        (per_group, u_share, units),
        (per_group, u_share, step_width),
        (per_group, 1, step_width),
        (per_group, 1, LANES),
    ]
    operands = (embed, conv_weight, trunk_in, trunk_mid, head, scale)
    return pl.pallas_call(
        partial(grad_kernel, (steps, feats, acts, n_dp)),
        grid=(per_group,),
        in_specs=[
            pl.BlockSpec(memory_space=pltpu.SMEM),
            pl.BlockSpec(slots.shape, lambda m: (0, 0)),
        ]
        + [per_member(x.shape) for x in operands],
        out_specs=[per_member(s) for s in out_shapes],
        out_shape=[jax.ShapeDtypeStruct(s, f32) for s in out_shapes],
        scratch_shapes=[
            pltpu.VMEM((room, slots.shape[1]), bf16),
            pltpu.VMEM((layers, 2 * channels, channels), bf16),
            pltpu.VMEM((layers, channels, 2 * channels), bf16),
            pltpu.VMEM((channels, units), bf16),
            pltpu.VMEM((units, units), bf16),
            pltpu.VMEM((layers + 1, tokens, channels), bf16),
            pltpu.VMEM((tokens, units), bf16),
            pltpu.VMEM((tokens, units), bf16),
            pltpu.VMEM((layers, tokens, channels), bf16),
            pltpu.VMEM((tokens, units), bf16),
            pltpu.VMEM((tokens, units), bf16),
            pltpu.VMEM((layers, c_width, 2 * channels), f32),
            pltpu.VMEM((c_width, units), f32),
            pltpu.VMEM((u_width, units), f32),
            pltpu.VMEM((u_width, step_width), f32),
            pltpu.VMEM((step_width, channels), f32),
            pltpu.VMEM((1, step_width), f32),
        ],
        compiler_params=pltpu.CompilerParams(vmem_limit_bytes=56 * 2**20),
    )(index, slots, *operands)


def local(
    observations,
    rollout,
    done_flags,
    member_ids,
    embed_weight,
    conv_weight,
    trunk_in,
    trunk_mid,
    head_weight,
    log_std,
):
    groups = lax.axis_size("member")
    per_group = embed_weight.shape[0]
    members = groups * per_group
    local_rows, steps = done_flags.shape
    feats, acts = embed_weight.shape[1], log_std.shape[1]
    capacity = 3 * local_rows // members * per_group
    rows = jnp.concatenate(
        [
            observations.reshape(local_rows, steps, -1),
            rollout.reshape(local_rows, steps, -1),
        ],
        axis=2,
    ).reshape(local_rows, -1)
    rows = jnp.concatenate(
        [
            rows,
            done_flags.astype(bf16),
            member_ids.astype(bf16),
            jnp.ones((local_rows, 1), bf16),
            jnp.zeros((local_rows, LANES - steps - 2), bf16),
        ],
        axis=1,
    )
    rows = lax.all_gather(rows, "dp", axis=0, tiled=True)
    owner_ids = rows[:, rows.shape[1] - LANES + steps].astype(jnp.int32)
    capacity = capacity * lax.axis_size("dp")
    group_ids = owner_ids // per_group
    same = group_ids[:, None] == group_ids[None, :]
    place = jnp.arange(rows.shape[0], dtype=jnp.int32)
    ranking = jnp.sum((same & (place[:, None] > place[None, :])).astype(jnp.int32), axis=1)
    target = group_ids * capacity + ranking
    dispatch = (jnp.arange(groups * capacity, dtype=jnp.int32)[:, None] == target[None, :]).astype(
        bf16
    )
    sent = dot(dispatch, rows).astype(bf16).reshape(groups, capacity, -1)
    received = lax.all_to_all(sent, "member", split_axis=0, concat_axis=0, tiled=True)
    slots = received.reshape(groups * capacity, -1)

    weights = (embed_weight, conv_weight, trunk_in, trunk_mid, head_weight, log_std)
    g_embed, g_conv, g_first, g_second, g_head, g_std, g_square = member_gradients(
        slots, steps, weights
    )
    entries = sum(math.prod(tensor.shape[1:]) for tensor in weights)
    squares = lax.psum(g_square[:, 0, 0], "dp")
    root_mean = jnp.sqrt(squares / entries + 1e-06)
    share = feats // lax.axis_size("dp")
    g_embed = lax.dynamic_slice_in_dim(g_embed, lax.axis_index("dp") * share, share, 1)
    g_head = g_head[:, :, feats : feats + acts + 1]
    g_std = g_std[:, 0, feats : feats + acts]
    return tuple(
        part / root_mean.reshape((-1,) + (1,) * (part.ndim - 1))
        for part in (g_embed, g_conv, g_first, g_second, g_head, g_std)
    )


def solution(mesh):
    placed = (
        P(("member", "dp"), None),
        P(("member", "dp"), None),
        P(("member", "dp"), None),
        P(("member", "dp"), None),
        P("member", None, None),
        P("member", None, None, None, None),
        P("member", None, None),
        P("member", None, None),
        P("member", None, None),
        P("member", None),
    )
    return jax.shard_map(
        local,
        mesh=mesh,
        in_specs=placed,
        out_specs=(
            P("member", "dp", None),
            P("member", None, None, "dp", None),
            P("member", "dp", None),
            P("member", "dp", None),
            P("member", "dp", None),
            P("member", None),
        ),
        check_vma=False,
    )
```

```python
from functools import partial
import math

import jax
import jax.numpy as jnp
from jax import lax
from jax.experimental import pallas as pl
from jax.experimental.pallas import tpu as pltpu
from jax.sharding import PartitionSpec as P

gamma_rate = 0.99
trace_rate = 0.95
half_log_tau = 0.9189385332046727

f32, bf16 = jnp.float32, jnp.bfloat16
LANES = 128
SPANS = 64


def dot(a, b):
    return jnp.dot(a, b, preferred_element_type=f32)


def dot_nt(a, b):
    return lax.dot_general(a, b, (((1,), (1,)), ((), ())), preferred_element_type=f32)


def dot_tn(a, b):
    return lax.dot_general(a, b, (((0,), (0,)), ((), ())), preferred_element_type=f32)


def elu_parts(p):
    slope = jnp.exp(jnp.minimum(p, 0.0))
    return jnp.maximum(p, 0.0) + (slope - 1.0), slope.astype(bf16)


def later(x, rows):
    return jnp.concatenate([jnp.zeros((rows, x.shape[1]), x.dtype), x[: x.shape[0] - rows]], axis=0)


def sooner(x, rows):
    return jnp.concatenate([x[rows:], jnp.zeros((rows, x.shape[1]), x.dtype)], axis=0)


def part_of(index, share):
    if share >= LANES:
        return pl.multiple_of(index * share, LANES), share, 0
    start = index * share
    whole = (start // LANES) * LANES
    return pl.multiple_of(whole, LANES), LANES, pl.multiple_of(start - whole, 8)


def grad_kernel(
    sizes,
    dp_ref,
    slots_ref,
    embed_ref,
    conv_ref,
    first_ref,
    second_ref,
    head_ref,
    std_ref,
    g_embed,
    g_conv,
    g_first,
    g_second,
    g_head,
    g_std,
    g_square,
    packed,
    w_conv,
    w_back,
    w_first,
    w_second,
    saved_hidden,
    saved_first,
    saved_second,
    slopes_conv,
    slopes_first,
    slopes_second,
    a_conv,
    a_first,
    a_second,
    a_head,
    a_embed,
    a_std,
):
    steps, feats, acts, n_dp = sizes
    member = pl.program_id(0)
    index = dp_ref[0]
    slot_count = slots_ref.shape[0]
    step_width = embed_ref.shape[1]
    channels = embed_ref.shape[2]
    units = first_ref.shape[2]
    layers = conv_ref.shape[1]
    room = packed.shape[0]
    tokens = steps * SPANS
    c_start, c_width, c_off = part_of(index, channels // n_dp)
    u_start, u_width, u_off = part_of(index, units // n_dp)

    tail = slots_ref[:, steps * step_width :]
    lanes = lax.broadcasted_iota(jnp.int32, (16, LANES), 1)
    owner = dot_nt((lanes == steps).astype(bf16), tail)
    used = dot_nt((lanes == steps + 1).astype(bf16), tail)
    wanted = (dp_ref[1] + member).astype(f32)
    mine = jnp.where((owner == wanted) & (used > 0.5), 1.0, 0.0).astype(bf16)
    upto = (
        lax.broadcasted_iota(jnp.int32, (slot_count, slot_count), 0)
        <= lax.broadcasted_iota(jnp.int32, (slot_count, slot_count), 1)
    ).astype(bf16)
    place = jnp.where(mine > 0, dot(mine, upto) - 1.0, -1.0)[:1]
    count = jnp.max(place).astype(jnp.int32) + 1
    choose = (
        lax.broadcasted_iota(jnp.int32, (room, slot_count), 0) == place.astype(jnp.int32)
    ).astype(bf16)
    packed[...] = dot(choose, slots_ref[...]).astype(bf16)

    w_embed = embed_ref[0].astype(bf16)
    w_head = head_ref[0].astype(bf16)
    for layer in range(layers):
        w_conv[layer, :channels] = conv_ref[0, layer, 0].astype(bf16)
        w_conv[layer, channels:] = conv_ref[0, layer, 1].astype(bf16)
        w_back[layer, :, :channels] = conv_ref[0, layer, 0].astype(bf16)
        w_back[layer, :, channels:] = conv_ref[0, layer, 1].astype(bf16)
    w_first[...] = first_ref[0].astype(bf16)
    w_second[...] = second_ref[0].astype(bf16)
    for total in (a_conv, a_first, a_second, a_head, a_embed, a_std):
        total[...] = jnp.zeros_like(total)
    scale = std_ref[0]
    inverse = jnp.exp(-scale)

    lane = lax.broadcasted_iota(jnp.int32, (1, step_width), 1)
    is_act = (lane >= feats) & (lane < feats + acts)
    value_lane = feats + acts

    def block(number, unused):
        row = pl.multiple_of(number * SPANS, SPANS)
        spans = packed[pl.ds(row, SPANS), :]
        tok = jnp.concatenate(
            [spans[:, t * step_width : (t + 1) * step_width] for t in range(steps)], axis=0
        )
        hidden = dot(tok, w_embed)
        for layer in range(layers):
            current = hidden.astype(bf16)
            saved_hidden[layer] = current
            both = jnp.concatenate([current, later(current, SPANS * 2**layer)], axis=1)
            grown, slope = elu_parts(dot(both, w_conv[layer]))
            slopes_conv[layer] = slope
            hidden = hidden + grown
        saved_hidden[layers] = hidden.astype(bf16)
        grown, slope = elu_parts(dot(saved_hidden[layers], w_first[...]))
        slopes_first[...] = slope
        saved_first[...] = grown.astype(bf16)
        grown, slope = elu_parts(dot(saved_first[...], w_second[...]))
        slopes_second[...] = slope
        saved_second[...] = grown.astype(bf16)
        out = dot(saved_second[...], w_head)

        record = tok.astype(f32)
        scaled = jnp.where(is_act, (record - out) * inverse, 0.0)
        logp = jnp.sum(-0.5 * scaled * scaled - scale, axis=1, keepdims=True) - acts * half_log_tau
        ratio = jnp.exp(logp - record[:, value_lane + 3 : value_lane + 4])
        old_value = record[:, value_lane + 1 : value_lane + 2]
        done = spans[:, steps * step_width :].astype(f32)
        alive = 1.0 - jnp.concatenate([done[:, t : t + 1] for t in range(steps)], axis=0)
        td_error = (
            record[:, value_lane : value_lane + 1]
            + gamma_rate * alive * record[:, value_lane + 2 : value_lane + 3]
            - old_value
        )
        carry = gamma_rate * trace_rate * alive
        running = td_error[(steps - 1) * SPANS :]
        columns = [running]
        for t in range(steps - 2, -1, -1):
            at = slice(t * SPANS, (t + 1) * SPANS)
            running = td_error[at] + carry[at] * running
            columns.append(running)
        advantage = jnp.concatenate(columns[::-1], axis=0)
        live = (
            lax.rem(lax.broadcasted_iota(jnp.int32, (tokens, 1), 0), SPANS) + number * SPANS < count
        )
        d_logp = jnp.where(live, 0.5 * (ratio - 1.0) - ratio * advantage, 0.0)
        d_value = jnp.where(
            live, 0.5 * (out[:, value_lane : value_lane + 1] - (advantage + old_value)), 0.0
        )
        d_out = jnp.where(
            is_act, d_logp * scaled * inverse, jnp.where(lane == value_lane, d_value, 0.0)
        ).astype(bf16)
        a_std[...] += jnp.sum(
            jnp.where(is_act, d_logp * (scaled * scaled - 1.0), 0.0), axis=0, keepdims=True
        )

        a_head[...] += dot_tn(saved_second[:, pl.ds(u_start, u_width)], d_out)
        d_second = dot_nt(d_out, w_head).astype(bf16) * slopes_second[...]
        a_second[...] += dot_tn(saved_first[:, pl.ds(u_start, u_width)], d_second)
        d_first = dot_nt(d_second, w_second[...]).astype(bf16) * slopes_first[...]
        a_first[...] += dot_tn(saved_hidden[layers, :, pl.ds(c_start, c_width)], d_first)
        d_hidden = dot_nt(d_first, w_first[...])
        for layer in range(layers - 1, -1, -1):
            lag = SPANS * 2**layer
            d_mix = d_hidden.astype(bf16) * slopes_conv[layer]
            d_taps = jnp.concatenate([d_mix, sooner(d_mix, lag)], axis=1)
            a_conv[layer] += dot_tn(saved_hidden[layer, :, pl.ds(c_start, c_width)], d_taps)
            d_hidden = d_hidden + dot_nt(d_taps, w_back[layer])
        a_embed[...] += dot_tn(tok, d_hidden.astype(bf16))
        return unused

    lax.fori_loop(0, (count + SPANS - 1) // SPANS, block, 0)

    c_share, u_share = channels // n_dp, units // n_dp
    squares = jnp.zeros((), f32)

    def keep(ref, at, value):
        ref[at] = value
        return jnp.sum(value * value)

    for layer in range(layers):
        for tap in range(2):
            columns = slice(tap * channels, (tap + 1) * channels)
            part = a_conv[layer, pl.ds(c_off, c_share), columns]
            squares += keep(g_conv, (0, layer, tap), part)
    squares += keep(g_first, 0, a_first[pl.ds(c_off, c_share), :])
    squares += keep(g_second, 0, a_second[pl.ds(u_off, u_share), :])
    squares += keep(g_head, 0, a_head[pl.ds(u_off, u_share), :])
    shared = keep(g_embed, 0, a_embed[:feats, :]) + keep(g_std, 0, a_std[...])
    g_square[...] = jnp.full(g_square.shape, squares + shared / n_dp, f32)


def member_gradients(slots, steps, weights):
    embed_weight, conv_weight, trunk_in, trunk_mid, head_weight, log_std = weights
    n_dp = lax.axis_size("dp")
    per_group, feats, channels = embed_weight.shape
    index = jnp.stack([lax.axis_index("dp"), lax.axis_index("member") * per_group]).astype(jnp.int32)
    layers, units, acts = conv_weight.shape[1], trunk_in.shape[2], log_std.shape[1]
    step_width = (slots.shape[1] - LANES) // steps
    fill = step_width - feats
    embed = jnp.pad(embed_weight, ((0, 0), (0, fill), (0, 0)))
    head = jnp.pad(head_weight, ((0, 0), (0, 0), (feats, fill - acts - 1)))
    scale = jnp.pad(log_std, ((0, 0), (feats, fill - acts)))[:, None, :]
    c_share, u_share = channels // n_dp, units // n_dp
    c_width, u_width = max(c_share, LANES), max(u_share, LANES)
    tokens = steps * SPANS
    room = -(-(slots.shape[0] // per_group) // SPANS) * SPANS

    def per_member(shape):
        zeros = (0,) * (len(shape) - 1)
        return pl.BlockSpec((1,) + tuple(shape[1:]), lambda m: (m,) + zeros)

    out_shapes = [
        (per_group, feats, channels),
        (per_group, layers, 2, c_share, channels),
        (per_group, c_share, units),
        (per_group, u_share, units),
        (per_group, u_share, step_width),
        (per_group, 1, step_width),
        (per_group, 1, LANES),
    ]
    operands = (embed, conv_weight, trunk_in, trunk_mid, head, scale)
    return pl.pallas_call(
        partial(grad_kernel, (steps, feats, acts, n_dp)),
        grid=(per_group,),
        in_specs=[
            pl.BlockSpec(memory_space=pltpu.SMEM),
            pl.BlockSpec(slots.shape, lambda m: (0, 0)),
        ]
        + [per_member(x.shape) for x in operands],
        out_specs=[per_member(s) for s in out_shapes],
        out_shape=[jax.ShapeDtypeStruct(s, f32) for s in out_shapes],
        scratch_shapes=[
            pltpu.VMEM((room, slots.shape[1]), bf16),
            pltpu.VMEM((layers, 2 * channels, channels), bf16),
            pltpu.VMEM((layers, channels, 2 * channels), bf16),
            pltpu.VMEM((channels, units), bf16),
            pltpu.VMEM((units, units), bf16),
            pltpu.VMEM((layers + 1, tokens, channels), bf16),
            pltpu.VMEM((tokens, units), bf16),
            pltpu.VMEM((tokens, units), bf16),
            pltpu.VMEM((layers, tokens, channels), bf16),
            pltpu.VMEM((tokens, units), bf16),
            pltpu.VMEM((tokens, units), bf16),
            pltpu.VMEM((layers, c_width, 2 * channels), f32),
            pltpu.VMEM((c_width, units), f32),
            pltpu.VMEM((u_width, units), f32),
            pltpu.VMEM((u_width, step_width), f32),
            pltpu.VMEM((step_width, channels), f32),
            pltpu.VMEM((1, step_width), f32),
        ],
        compiler_params=pltpu.CompilerParams(vmem_limit_bytes=56 * 2**20),
    )(index, slots, *operands)


def local(
    observations,
    rollout,
    done_flags,
    member_ids,
    embed_weight,
    conv_weight,
    trunk_in,
    trunk_mid,
    head_weight,
    log_std,
):
    groups = lax.axis_size("member")
    per_group = embed_weight.shape[0]
    members = groups * per_group
    local_rows, steps = done_flags.shape
    feats, acts = embed_weight.shape[1], log_std.shape[1]
    capacity = 3 * local_rows // members * per_group
    rows = jnp.concatenate(
        [
            observations.reshape(local_rows, steps, -1),
            rollout.reshape(local_rows, steps, -1),
        ],
        axis=2,
    ).reshape(local_rows, -1)
    rows = jnp.concatenate(
        [
            rows,
            done_flags.astype(bf16),
            member_ids.astype(bf16),
            jnp.ones((local_rows, 1), bf16),
            jnp.zeros((local_rows, LANES - steps - 2), bf16),
        ],
        axis=1,
    )
    rows = lax.all_gather(rows, "dp", axis=0, tiled=True)
    owner_ids = rows[:, rows.shape[1] - LANES + steps].astype(jnp.int32)
    capacity = capacity * lax.axis_size("dp")
    group_ids = owner_ids // per_group
    same = group_ids[:, None] == group_ids[None, :]
    place = jnp.arange(rows.shape[0], dtype=jnp.int32)
    ranking = jnp.sum((same & (place[:, None] > place[None, :])).astype(jnp.int32), axis=1)
    target = group_ids * capacity + ranking
    dispatch = (jnp.arange(groups * capacity, dtype=jnp.int32)[:, None] == target[None, :]).astype(
        bf16
    )
    sent = dot(dispatch, rows).astype(bf16).reshape(groups, capacity, -1)
    received = lax.all_to_all(sent, "member", split_axis=0, concat_axis=0, tiled=True)
    slots = received.reshape(groups * capacity, -1)

    weights = (embed_weight, conv_weight, trunk_in, trunk_mid, head_weight, log_std)
    g_embed, g_conv, g_first, g_second, g_head, g_std, g_square = member_gradients(
        slots, steps, weights
    )
    entries = sum(math.prod(tensor.shape[1:]) for tensor in weights)
    squares = lax.psum(g_square[:, 0, 0], "dp")
    root_mean = jnp.sqrt(squares / entries + 1e-06)
    share = feats // lax.axis_size("dp")
    g_embed = lax.dynamic_slice_in_dim(g_embed, lax.axis_index("dp") * share, share, 1)
    g_head = g_head[:, :, feats : feats + acts + 1]
    g_std = g_std[:, 0, feats : feats + acts]
    return tuple(
        part / root_mean.reshape((-1,) + (1,) * (part.ndim - 1))
        for part in (g_embed, g_conv, g_first, g_second, g_head, g_std)
    )


def solution(mesh):
    placed = (
        P(("member", "dp"), None),
        P(("member", "dp"), None),
        P(("member", "dp"), None),
        P(("member", "dp"), None),
        P("member", None, None),
        P("member", None, None, None, None),
        P("member", None, None),
        P("member", None, None),
        P("member", None, None),
        P("member", None),
    )
    return jax.shard_map(
        local,
        mesh=mesh,
        in_specs=placed,
        out_specs=(
            P("member", "dp", None),
            P("member", None, None, "dp", None),
            P("member", "dp", None),
            P("member", "dp", None),
            P("member", "dp", None),
            P("member", None),
        ),
        check_vma=False,
    )
```
